32 devices in a mesh: groups: 2 (over x), chan: 16 (over z, y, core).
Axes of the slice: x: 2, y: 2, z: 4, core: 2. Of those that a mesh axis runs over, the one named last changes fastest.
Arguments:
- raw_strain: bfloat16 [8, 512, 4096], P(None, ('groups', 'chan')), parts along dimension 1, may hold values from -60 to 60
- bandpass: bfloat16 [64], replicated, may hold values from -0.75 to 0.75
- whiten_taps: bfloat16 [512, 64], P(('groups', 'chan')), parts along dimension 0, may hold values from -0.75 to 0.75
- segment_mask: int32 [8, 512], P(None, 'groups'), parts along dimension 1, may hold values from 0 to 1, as said below
- channel_block: int32 [512], P('groups'), parts along dimension 0, may hold values from 0 to 1, as said below
- source_block: int32 [2], P('groups'), parts along dimension 0, may hold values from 0 to 1
Outputs:
- correlations: bfloat16 [128, 512, 1024], P(None, ('groups', 'chan')), parts along dimension 1
The draws below stay inside these ranges and needn't reach their ends.
There are 2 independent parts, one for each index of `groups`. The reference program is written for one: setup_inputs(seed, part) draws one part's arguments, and reference() takes and returns one part's arrays. A program takes and returns all parts, laid end to end along the dimension named above; an argument that names none is the same for every part. Nothing has to cross between parts.
Inputs may be any that keep to these rules, and one draw needn't show every extreme that they name: `segment_mask`: 1 marks a usable segment of a channel; some channels have no usable segment. `channel_block`: each block number is held by exactly 128 channels.
All inputs are finite; a program needn't handle non-finite values.
Results may differ from the reference program's by a relative error of at most 0.0093.
Values may be sent and summed in bfloat16 or wider, within the bound.
A program may use at most 64 MiB of HBM per device.

```python
import math
import jax
import jax.numpy as jnp
from jax import lax

SAMPLES = 4096
TAPS = 64
KLO = 64
FBINS = 512
LAGS = 1024
BLOCK = 128
SEGS = 8
CHANNELS = 256


def draw_raw_strain(key, part):
    noise_key, level_key = jax.random.split(key)
    noise = jnp.clip(jax.random.normal(noise_key, (SEGS, CHANNELS, SAMPLES), jnp.float32), -6.0, 6.0)
    level = jnp.exp(jax.random.uniform(level_key, (SEGS, CHANNELS, 1), jnp.float32, 0.0, math.log(10.0)))
    return (noise * level).astype(jnp.bfloat16)


def draw_segment_mask(key, part):
    usable_key, alive_key, dead_key = jax.random.split(key, 3)
    usable = jax.random.randint(usable_key, (SEGS, CHANNELS), 0, 4) > 0
    alive = jax.random.randint(alive_key, (1, CHANNELS), 0, 16) > 0
    dead_one = jax.random.randint(dead_key, (), 0, CHANNELS)
    alive = alive & (jnp.arange(CHANNELS, dtype=jnp.int32)[None, :] != dead_one)
    return (usable & alive).astype(jnp.int32)


def draw_channel_block(key, part):
    return (jax.random.permutation(key, CHANNELS) // BLOCK).astype(jnp.int32)


def block_scale(rng, shape, cuts, least, largest):
    factor_of, own = 1.0, jax.random.fold_in(rng, 6)
    for dim, shards_of in cuts:
        heights = jnp.exp(jax.random.uniform(jax.random.fold_in(own, dim), (shards_of,), jnp.float32, least / len(cuts), largest / len(cuts)))
        factor_of = factor_of * jnp.repeat(heights, shape[dim] // shards_of).reshape([-1 if axis == dim else 1 for axis in range(len(shape))])
    return factor_of


def normal_values(stream_key, shape, scale, bound, cuts=(), held_as=jnp.bfloat16):
    values = jax.random.normal(stream_key, shape, jnp.float32) * scale
    if len(cuts) > 0:
        values = block_scale(stream_key, shape, cuts, -0.22, 0.18) * values
    return jnp.clip(values, min=-bound, max=bound).astype(held_as)


def setup_inputs(seed: int = 0, part: int = 0) -> dict:
    key_list = jax.random.split(jax.random.key(seed), 7)
    part_keys = jax.random.split(jax.random.fold_in(key_list[6], part), 7)
    return {
        "raw_strain": draw_raw_strain(jax.random.fold_in(jax.random.fold_in(key_list[6], part), 71), part),
        "bandpass": normal_values(key_list[1], (TAPS,), TAPS ** -0.5, 0.75),
        "whiten_taps": normal_values(part_keys[2], (CHANNELS, TAPS), TAPS ** -0.5, 0.75, ((0, 16),)),
        "segment_mask": draw_segment_mask(jax.random.fold_in(jax.random.fold_in(key_list[6], part), 71), part),
        "channel_block": draw_channel_block(jax.random.fold_in(jax.random.fold_in(key_list[6], part), 71), part),
        "source_block": jax.random.randint(part_keys[5], (1,), 0, CHANNELS // BLOCK).astype(jnp.int32),
    }


def fir_matrix(coeffs):
    inner_idx = jnp.arange(256, dtype=jnp.int32)[:, None]
    outer_idx = jnp.arange(128, dtype=jnp.int32)[None, :]
    offset = outer_idx + 128 - inner_idx
    inside = (offset >= 0) & (offset < coeffs.shape[-1])
    picked = jnp.take(coeffs, jnp.clip(offset, 0, coeffs.shape[-1] - 1), axis=-1)
    return jnp.where(inside, picked, jnp.zeros_like(picked))

def fir_pass(signal, matrix, einsum_form):
    blocks = signal.reshape(signal.shape[:-1] + (signal.shape[-1] // 128, 128))
    joined = jnp.concatenate([jnp.roll(blocks, 1, axis=-2), blocks], axis=-1)
    result = jnp.einsum(einsum_form, joined.astype(jnp.float32), matrix.astype(jnp.float32), precision=lax.Precision.HIGHEST)
    return result.reshape(signal.shape)

def reference(raw_strain, bandpass, whiten_taps, segment_mask, channel_block, source_block):
    filtered = fir_pass(raw_strain, fir_matrix(bandpass), 'gcbi,io->gcbo')
    energy = lax.optimization_barrier(jnp.mean(filtered * filtered, axis=-1, keepdims=True))
    normalized = (filtered / jnp.sqrt(energy + 1e-05)).astype(jnp.bfloat16)
    whitened = fir_pass(normalized, fir_matrix(whiten_taps), 'gcbi,cio->gcbo').astype(jnp.bfloat16)
    bin_index = KLO + jnp.arange(FBINS, dtype=jnp.int32)
    sample_idx = jnp.arange(SAMPLES, dtype=jnp.int32)
    phase_idx = sample_idx[:, None] * bin_index[None, :] % SAMPLES
    angles = phase_idx.astype(jnp.float32) * (2.0 * math.pi / SAMPLES)
    dft_table = jnp.concatenate([jnp.cos(angles).astype(jnp.bfloat16), (-jnp.sin(angles)).astype(jnp.bfloat16)], axis=1)
    spectra = jnp.dot(whitened.reshape(-1, SAMPLES).astype(jnp.float32), dft_table.astype(jnp.float32), precision=lax.Precision.HIGHEST)
    mask_all = segment_mask.astype(jnp.float32)
    spectra = spectra.reshape(SEGS, CHANNELS, 2, FBINS) * mask_all[:, :, None, None]
    spectra = spectra.astype(jnp.bfloat16).astype(jnp.float32)
    member = channel_block == source_block[0]
    member_rank = jnp.cumsum(member.astype(jnp.int32)) - 1
    chosen = member[None, :] & (member_rank[None, :] == jnp.arange(BLOCK, dtype=jnp.int32)[:, None])
    selector = chosen.astype(jnp.float32)
    sources = jnp.einsum('sc,gckf->gskf', selector, spectra, precision=lax.Precision.HIGHEST)
    turned = jnp.stack([-sources[:, :, 1], sources[:, :, 0]], axis=2)
    paired = jnp.stack([sources, turned], axis=0)
    stacked = jnp.einsum('jgskf,grkf->srjf', paired, spectra, precision=lax.Precision.HIGHEST)
    stacked = stacked.astype(jnp.bfloat16)
    source_mask = jnp.dot(mask_all, selector.T, precision=lax.Precision.HIGHEST)
    counts = jnp.dot(source_mask.T, mask_all, precision=lax.Precision.HIGHEST)
    lag_index = jnp.arange(LAGS, dtype=jnp.int32) - LAGS // 2
    lag_phase = bin_index[:, None] * lag_index[None, :] % SAMPLES
    lag_angles = lag_phase.astype(jnp.float32) * (2.0 * math.pi / SAMPLES)
    lag_table = jnp.concatenate([jnp.cos(lag_angles).astype(jnp.bfloat16), (-jnp.sin(lag_angles)).astype(jnp.bfloat16)], axis=0)
    lagged = jnp.dot(stacked.reshape(BLOCK * CHANNELS, 2 * FBINS).astype(jnp.float32), lag_table.astype(jnp.float32), precision=lax.Precision.HIGHEST)
    lagged = lagged.reshape(BLOCK, CHANNELS, LAGS)
    factor = 2.0 / (SAMPLES * math.sqrt(FBINS))
    return (lagged * factor / jnp.maximum(counts, 1.0)[:, :, None]).astype(jnp.bfloat16)
```

```python
import math

import jax
import numpy as np
import jax.numpy as jnp
from jax import lax
from jax.sharding import PartitionSpec as P

SAMPLES = 4096
KLO = 64
FBINS = 512
LAGS = 1024
BLOCK = 128


def table(phase):
    angles = phase.astype(np.float32) * np.float32(2.0 * math.pi / SAMPLES)
    return np.cos(angles).astype(jnp.bfloat16), (-np.sin(angles)).astype(jnp.bfloat16)


def dft_table():
    bins = KLO + np.arange(FBINS)
    return np.concatenate(table(np.arange(SAMPLES)[:, None] * bins[None, :] % SAMPLES), axis=1)


def lag_table_np():
    bins = KLO + np.arange(FBINS)
    return np.concatenate(table(bins[:, None] * (np.arange(LAGS) - LAGS // 2)[None, :] % SAMPLES), axis=0)


def fir_matrix(coeffs):
    inner_idx = jnp.arange(256, dtype=jnp.int32)[:, None]
    outer_idx = jnp.arange(128, dtype=jnp.int32)[None, :]
    offset = outer_idx + 128 - inner_idx
    inside = (offset >= 0) & (offset < coeffs.shape[-1])
    picked = jnp.take(coeffs, jnp.clip(offset, 0, coeffs.shape[-1] - 1), axis=-1)
    return jnp.where(inside, picked, jnp.zeros_like(picked))


def fir_pass(signal, matrix, einsum_form):
    blocks = signal.reshape(signal.shape[:-1] + (signal.shape[-1] // 128, 128))
    joined = jnp.concatenate([jnp.roll(blocks, 1, axis=-2), blocks], axis=-1)
    result = jnp.einsum(einsum_form, joined, matrix, preferred_element_type=jnp.float32)
    return result.reshape(signal.shape)


def cross_stack(sources, receivers):
    turned = jnp.stack([-sources[:, :, 1], sources[:, :, 0]], axis=2)
    paired = jnp.stack([sources, turned], axis=0)
    return jnp.einsum("jgskf,grkf->srjf", paired, receivers, preferred_element_type=jnp.float32)


def body(raw_strain, bandpass, whiten_taps, segment_mask, channel_block, source_block):
    seg_count, chan_rows, sample_count = raw_strain.shape
    chan_start = lax.axis_index("chan") * chan_rows
    mask_all = segment_mask.astype(jnp.float32)
    mask_here = lax.dynamic_slice_in_dim(mask_all, chan_start, chan_rows, 1)
    filtered = fir_pass(raw_strain, fir_matrix(bandpass), "gcbi,io->gcbo")
    energy = jnp.mean(filtered * filtered, axis=-1, keepdims=True)
    normalized = (filtered / jnp.sqrt(energy + 1e-05)).astype(jnp.bfloat16)
    whitened = fir_pass(normalized, fir_matrix(whiten_taps), "gcbi,cio->gcbo").astype(jnp.bfloat16)
    time_rows = whitened.reshape(seg_count * chan_rows, sample_count)
    spectra = jnp.dot(time_rows, jnp.asarray(dft_table()), preferred_element_type=jnp.float32)
    spectra = (
        spectra.reshape(seg_count, chan_rows, 2, FBINS) * mask_here[:, :, None, None]
    ).astype(jnp.bfloat16)
    member = channel_block == source_block[0]
    order = jnp.arange(member.shape[0], dtype=jnp.int32)
    below = member[None, :] & (order[None, :] < order[:, None])
    member_rank = jnp.sum(below.astype(jnp.int32), axis=1)
    chosen = member[None, :] & (member_rank[None, :] == jnp.arange(BLOCK, dtype=jnp.int32)[:, None])
    selector = chosen.astype(jnp.bfloat16)
    source_mask = jnp.dot(mask_all, chosen.astype(jnp.float32).T)
    counts = jnp.dot(source_mask.T, mask_here)
    sources = jnp.einsum(
        "sc,gckf->gskf",
        selector,
        lax.all_gather(spectra, "chan", axis=1, tiled=True),
        preferred_element_type=jnp.float32,
    ).astype(jnp.bfloat16)
    stacked = cross_stack(sources, spectra).astype(jnp.bfloat16)
    lag_table = jnp.asarray(lag_table_np())
    lagged = jnp.dot(
        stacked.reshape(BLOCK * chan_rows, 2 * FBINS), lag_table, preferred_element_type=jnp.float32
    )
    lagged = lagged.reshape(BLOCK, chan_rows, LAGS)
    factor = 2.0 / (SAMPLES * math.sqrt(FBINS))
    return (lagged * factor / jnp.maximum(counts, 1.0)[:, :, None]).astype(jnp.bfloat16)


def solution(mesh):
    in_specs = (
        P(None, ("groups", "chan"), None),
        P(),
        P(("groups", "chan"), None),
        P(None, "groups"),
        P("groups"),
        P("groups"),
    )
    out_specs = P(None, ("groups", "chan"), None)
    return jax.shard_map(body, mesh=mesh, in_specs=in_specs, out_specs=out_specs, check_vma=False)
```

```python
import math

import jax
import numpy as np
import jax.numpy as jnp
from jax import lax
from jax.experimental import pallas as pl
from jax.experimental.pallas import tpu as pltpu
from jax.sharding import PartitionSpec as P

SAMPLES = 4096
KLO = 64
FBINS = 512
LAGS = 1024
BLOCK = 128


def table(phase):
    angles = phase.astype(np.float32) * np.float32(2.0 * math.pi / SAMPLES)
    return np.cos(angles).astype(jnp.bfloat16), (-np.sin(angles)).astype(jnp.bfloat16)


def dft_table():
    bins = KLO + np.arange(FBINS)
    return np.concatenate(table(np.arange(SAMPLES)[:, None] * bins[None, :] % SAMPLES), axis=1)


def lag_table_np():
    bins = KLO + np.arange(FBINS)
    return np.concatenate(table(bins[:, None] * (np.arange(LAGS) - LAGS // 2)[None, :] % SAMPLES), axis=0)


def toeplitz(taps):
    turned = pltpu.roll(jnp.broadcast_to(taps, (128, 128)), 0, 1, stride=1, stride_axis=0)
    row = lax.broadcasted_iota(jnp.int32, (128, 128), 0)
    lane = lax.broadcasted_iota(jnp.int32, (128, 128), 1)
    before = jnp.where(lane < row, turned, 0.0)
    here = jnp.where(lane >= row, turned, 0.0)
    return jnp.concatenate([before, here], axis=0).astype(jnp.bfloat16)


def front_kernel(raw_ref, band_ref, taps_ref, mask_ref, table_ref, out_ref, filt, inv, white, acc):
    segs, rows, samples = raw_ref.shape
    blocks = samples // 128
    step = pl.program_id(0)
    depth = table_ref.shape[0]

    @pl.when(step == 0)
    def _():
        matrix = toeplitz(band_ref[...])
        power = jnp.zeros((segs * rows, 128), jnp.float32)
        for b in range(blocks):
            if b == 0:
                joined = jnp.concatenate([raw_ref[:, :, samples - 128 :], raw_ref[:, :, :128]], axis=2)
            else:
                joined = raw_ref[:, :, (b - 1) * 128 : (b + 1) * 128]
            part = jnp.dot(joined.reshape(segs * rows, 256), matrix, preferred_element_type=jnp.float32)
            power = power + part * part
            filt[:, :, b * 128 : (b + 1) * 128] = part.reshape(segs, rows, 128)
        energy = jnp.sum(power, axis=1, keepdims=True) * (1.0 / samples)
        scale = 1.0 / jnp.sqrt(energy + 1e-05)
        inv[...] = jnp.broadcast_to(scale, (segs * rows, 128)).reshape(segs, rows, 128)
        for c in range(rows):
            matrix = toeplitz(taps_ref[c : c + 1, :])
            scale = inv[:, c, :]
            here = jnp.concatenate(
                [filt[:, c, b * 128 : (b + 1) * 128] * scale for b in range(blocks)], axis=0
            )
            before = jnp.concatenate([here[-segs:], here[:-segs]], axis=0)
            joined = jnp.concatenate([before, here], axis=1).astype(jnp.bfloat16)
            part = jnp.dot(joined, matrix, preferred_element_type=jnp.float32)
            for b in range(blocks):
                white[c * segs : (c + 1) * segs, b * 128 : (b + 1) * 128] = part[b * segs : (b + 1) * segs]
        acc[...] = jnp.zeros_like(acc)

    first = pl.multiple_of(step * depth, depth)
    acc[...] += jnp.dot(
        white[:, pl.ds(first, depth)].astype(jnp.bfloat16), table_ref[...], preferred_element_type=jnp.float32
    )

    @pl.when(step == pl.num_programs(0) - 1)
    def _():
        out_ref[...] = (acc[...] * mask_ref[...]).astype(jnp.bfloat16)


def front(raw, bandpass, whiten_taps, mask_here):
    segs, rows, samples = raw.shape
    pad = ((0, 0), (0, 128 - bandpass.shape[-1]))
    band = jnp.pad(bandpass.astype(jnp.float32)[None], pad)
    taps = jnp.pad(whiten_taps.astype(jnp.float32), pad)
    mask = mask_here.T.reshape(rows * segs, 1)
    depth = 512
    whole = lambda *shape: pl.BlockSpec(shape, lambda i: (0,) * len(shape))
    return pl.pallas_call(
        front_kernel,
        grid=(samples // depth,),
        out_shape=jax.ShapeDtypeStruct((rows * segs, 2 * FBINS), jnp.bfloat16),
        in_specs=[
            whole(segs, rows, samples),
            whole(1, 128),
            whole(rows, 128),
            whole(rows * segs, 1),
            pl.BlockSpec((depth, 2 * FBINS), lambda i: (i, 0)),
        ],
        out_specs=whole(rows * segs, 2 * FBINS),
        scratch_shapes=[
            pltpu.VMEM((segs, rows, samples), jnp.float32),
            pltpu.VMEM((segs, rows, 128), jnp.float32),
            pltpu.VMEM((rows * segs, samples), jnp.float32),
            pltpu.VMEM((rows * segs, 2 * FBINS), jnp.float32),
        ],
        compiler_params=pltpu.CompilerParams(vmem_limit_bytes=40 * 2**20),
        cost_estimate=pl.CostEstimate(flops=2 * 10**9, bytes_accessed=10**7, transcendentals=0),
    )(raw, band, taps, mask, jnp.asarray(dft_table()))


def cross_stack(sources, receivers):
    turned = jnp.stack([-sources[:, :, 1], sources[:, :, 0]], axis=2)
    paired = jnp.stack([sources, turned], axis=0)
    return jnp.einsum("jsgkf,rgkf->srjf", paired, receivers, preferred_element_type=jnp.float32)


def body(raw_strain, bandpass, whiten_taps, segment_mask, channel_block, source_block):
    seg_count, chan_rows, sample_count = raw_strain.shape
    chan_start = lax.axis_index("chan") * chan_rows
    mask_all = segment_mask.astype(jnp.float32)
    mask_here = lax.dynamic_slice_in_dim(mask_all, chan_start, chan_rows, 1)
    spectra = front(raw_strain, bandpass, whiten_taps, mask_here)
    gathered = lax.all_gather(spectra, "chan", axis=0, tiled=True).reshape(-1, seg_count, 2, FBINS)
    spectra = spectra.reshape(chan_rows, seg_count, 2, FBINS)
    member = channel_block == source_block[0]
    order = jnp.arange(member.shape[0], dtype=jnp.int32)
    below = member[None, :] & (order[None, :] < order[:, None])
    member_rank = jnp.sum(below.astype(jnp.int32), axis=1)
    chosen = member[None, :] & (member_rank[None, :] == jnp.arange(BLOCK, dtype=jnp.int32)[:, None])
    selector = chosen.astype(jnp.bfloat16)
    source_mask = jnp.dot(mask_all, chosen.astype(jnp.float32).T)
    counts = jnp.dot(source_mask.T, mask_here)
    sources = jnp.einsum(
        "sc,cgkf->sgkf",
        selector,
        gathered,
        preferred_element_type=jnp.float32,
    ).astype(jnp.bfloat16)
    stacked = cross_stack(sources, spectra).astype(jnp.bfloat16)
    lag_table = jnp.asarray(lag_table_np())
    lagged = jnp.dot(
        stacked.reshape(BLOCK * chan_rows, 2 * FBINS), lag_table, preferred_element_type=jnp.float32
    )
    lagged = lagged.reshape(BLOCK, chan_rows, LAGS)
    factor = 2.0 / (SAMPLES * math.sqrt(FBINS))
    return (lagged * factor / jnp.maximum(counts, 1.0)[:, :, None]).astype(jnp.bfloat16)


def solution(mesh):
    in_specs = (
        P(None, ("groups", "chan"), None),
        P(),
        P(("groups", "chan"), None),
        P(None, "groups"),
        P("groups"),
        P("groups"),
    )
    out_specs = P(None, ("groups", "chan"), None)
    return jax.shard_map(body, mesh=mesh, in_specs=in_specs, out_specs=out_specs, check_vma=False)
```

```python
import functools
import math

import jax
import numpy as np
import jax.numpy as jnp
from jax import lax
from jax.experimental import pallas as pl
from jax.experimental.pallas import tpu as pltpu
from jax.sharding import PartitionSpec as P

SAMPLES = 4096
KLO = 64
FBINS = 512
LAGS = 1024
BLOCK = 128


def table(phase):
    angles = phase.astype(np.float32) * np.float32(2.0 * math.pi / SAMPLES)
    return np.cos(angles).astype(jnp.bfloat16), (-np.sin(angles)).astype(jnp.bfloat16)


def dft_table():
    bins = KLO + np.arange(FBINS)
    return np.concatenate(table(np.arange(SAMPLES)[:, None] * bins[None, :] % SAMPLES), axis=1)


def lag_table_np():
    bins = KLO + np.arange(FBINS)
    return np.concatenate(table(bins[:, None] * (np.arange(LAGS) - LAGS // 2)[None, :] % SAMPLES), axis=0)


def toeplitz(taps):
    turned = pltpu.roll(jnp.broadcast_to(taps, (128, 128)), 0, 1, stride=1, stride_axis=0)
    row = lax.broadcasted_iota(jnp.int32, (128, 128), 0)
    lane = lax.broadcasted_iota(jnp.int32, (128, 128), 1)
    before = jnp.where(lane < row, turned, 0.0)
    here = jnp.where(lane >= row, turned, 0.0)
    return jnp.concatenate([before, here], axis=0).astype(jnp.bfloat16)


def front_kernel(raw_ref, band_ref, taps_ref, mask_ref, table_ref, out_ref, filt, inv, white, acc):
    segs, rows, samples = raw_ref.shape
    blocks = samples // 128
    step = pl.program_id(0)
    depth = table_ref.shape[0]

    @pl.when(step == 0)
    def _():
        matrix = toeplitz(band_ref[...])
        power = jnp.zeros((segs * rows, 128), jnp.float32)
        for b in range(blocks):
            if b == 0:
                joined = jnp.concatenate([raw_ref[:, :, samples - 128 :], raw_ref[:, :, :128]], axis=2)
            else:
                joined = raw_ref[:, :, (b - 1) * 128 : (b + 1) * 128]
            part = jnp.dot(joined.reshape(segs * rows, 256), matrix, preferred_element_type=jnp.float32)
            power = power + part * part
            filt[:, :, b * 128 : (b + 1) * 128] = part.reshape(segs, rows, 128)
        energy = jnp.sum(power, axis=1, keepdims=True) * (1.0 / samples)
        scale = 1.0 / jnp.sqrt(energy + 1e-05)
        inv[...] = jnp.broadcast_to(scale, (segs * rows, 128)).reshape(segs, rows, 128)
        for c in range(rows):
            matrix = toeplitz(taps_ref[c : c + 1, :])
            scale = inv[:, c, :]
            here = jnp.concatenate(
                [filt[:, c, b * 128 : (b + 1) * 128] * scale for b in range(blocks)], axis=0
            )
            before = jnp.concatenate([here[-segs:], here[:-segs]], axis=0)
            joined = jnp.concatenate([before, here], axis=1).astype(jnp.bfloat16)
            part = jnp.dot(joined, matrix, preferred_element_type=jnp.float32)
            for b in range(blocks):
                white[c * segs : (c + 1) * segs, b * 128 : (b + 1) * 128] = part[b * segs : (b + 1) * segs]
        acc[...] = jnp.zeros_like(acc)

    first = pl.multiple_of(step * depth, depth)
    acc[...] += jnp.dot(
        white[:, pl.ds(first, depth)].astype(jnp.bfloat16), table_ref[...], preferred_element_type=jnp.float32
    )

    @pl.when(step == pl.num_programs(0) - 1)
    def _():
        out_ref[...] = (acc[...] * mask_ref[...]).astype(jnp.bfloat16)


def front(raw, bandpass, whiten_taps, mask_here):
    segs, rows, samples = raw.shape
    pad = ((0, 0), (0, 128 - bandpass.shape[-1]))
    band = jnp.pad(bandpass.astype(jnp.float32)[None], pad)
    taps = jnp.pad(whiten_taps.astype(jnp.float32), pad)
    mask = mask_here.T.reshape(rows * segs, 1)
    depth = 512
    whole = lambda *shape: pl.BlockSpec(shape, lambda i: (0,) * len(shape))
    return pl.pallas_call(
        front_kernel,
        grid=(samples // depth,),
        out_shape=jax.ShapeDtypeStruct((rows * segs, 2 * FBINS), jnp.bfloat16),
        in_specs=[
            whole(segs, rows, samples),
            whole(1, 128),
            whole(rows, 128),
            whole(rows * segs, 1),
            pl.BlockSpec((depth, 2 * FBINS), lambda i: (i, 0)),
        ],
        out_specs=whole(rows * segs, 2 * FBINS),
        scratch_shapes=[
            pltpu.VMEM((segs, rows, samples), jnp.float32),
            pltpu.VMEM((segs, rows, 128), jnp.float32),
            pltpu.VMEM((rows * segs, samples), jnp.float32),
            pltpu.VMEM((rows * segs, 2 * FBINS), jnp.float32),
        ],
        compiler_params=pltpu.CompilerParams(vmem_limit_bytes=40 * 2**20),
        cost_estimate=pl.CostEstimate(flops=2 * 10**9, bytes_accessed=10**7, transcendentals=0),
    )(raw, band, taps, mask, jnp.asarray(dft_table()))


PIECES = 2


def gather_kernel(count, own_ref, out_ref, own_sem, up_sem, down_sem, y_sem, core_sem, recv_sem):
    levels = count // 4
    me = lax.axis_index("chan")
    level, side, core = me // 4, (me // 2) % 2, me % 2
    y_peer = me + 2 - 4 * side
    core_peer = me + 1 - 2 * core
    has_up, has_down = level < levels - 1, level > 0
    barrier = pltpu.get_barrier_semaphore()

    def greet(peer):
        pl.semaphore_signal(barrier, inc=1, device_id={"chan": peer}, device_id_type=pl.DeviceIdType.MESH)

    greet(y_peer)
    greet(core_peer)

    @pl.when(has_up)
    def _():
        greet(me + 4)

    @pl.when(has_down)
    def _():
        greet(me - 4)

    pl.semaphore_wait(barrier, 2 + has_up.astype(jnp.int32) + has_down.astype(jnp.int32))

    height = own_ref.shape[0] // PIECES

    def send(block, piece, sems, peer, source=None):
        rows = pl.ds(piece * height, height)
        place = out_ref.at[block, rows]
        return pltpu.make_async_remote_copy(
            src_ref=place if source is None else source.at[rows],
            dst_ref=place,
            send_sem=sems.at[block, piece],
            recv_sem=recv_sem.at[block, piece],
            device_id={"chan": peer},
            device_id_type=pl.DeviceIdType.MESH,
        )

    def arrived(block, piece):
        send(block, piece, y_sem, y_peer).wait_recv()

    keep = pltpu.make_async_copy(own_ref, out_ref.at[me], own_sem)
    keep.start()
    for piece in range(PIECES):

        @pl.when(has_up)
        def _():
            send(me, piece, up_sem, me + 4, own_ref).start()

        @pl.when(has_down)
        def _():
            send(me, piece, down_sem, me - 4, own_ref).start()

        send(me, piece, y_sem, y_peer, own_ref).start()
        send(me, piece, core_sem, core_peer, own_ref).start()

    def across(far):
        for piece in range(PIECES):
            block = far * 4 + (1 - side) * 2 + core
            arrived(block, piece)
            send(block, piece, core_sem, core_peer).start()

    def each(distance, act):
        for way in (1, -1):
            far = level + way * distance
            if distance == 0 and way == -1:
                continue

            @pl.when((far >= 0) & (far < levels))
            def _():
                act(far, way)

    for distance in range(1, levels + 1):
        if distance < levels:

            def along(far, way):
                block = far * 4 + side * 2 + core
                for piece in range(PIECES):
                    arrived(block, piece)
                    if way == 1:

                        @pl.when(has_down)
                        def _():
                            send(block, piece, down_sem, me - 4).start()
                    else:

                        @pl.when(has_up)
                        def _():
                            send(block, piece, up_sem, me + 4).start()

                    send(block, piece, y_sem, y_peer).start()
                    send(block, piece, core_sem, core_peer).start()

            each(distance, along)
        each(distance - 1, lambda far, way: across(far))

    for far in range(levels):
        for piece in range(PIECES):
            mine, other = far * 4 + side * 2 + core, far * 4 + (1 - side) * 2 + core
            arrived(far * 4 + side * 2 + 1 - core, piece)
            arrived(far * 4 + (1 - side) * 2 + 1 - core, piece)
            send(mine, piece, y_sem, y_peer).wait_send()
            send(mine, piece, core_sem, core_peer).wait_send()
            send(other, piece, core_sem, core_peer).wait_send()

            @pl.when(has_up & (far <= level))
            def _():
                send(mine, piece, up_sem, me + 4).wait_send()

            @pl.when(has_down & (far >= level))
            def _():
                send(mine, piece, down_sem, me - 4).wait_send()

    keep.wait()


def gather(own, count):
    if count % 4 or count < 4:
        return lax.all_gather(own, "chan", axis=0)
    sems = pltpu.SemaphoreType.DMA((count, PIECES))
    return pl.pallas_call(
        lambda *refs: gather_kernel(count, *refs),
        out_shape=jax.ShapeDtypeStruct((count,) + own.shape, own.dtype),
        in_specs=[pl.BlockSpec(memory_space=pltpu.VMEM)],
        out_specs=pl.BlockSpec(memory_space=pltpu.VMEM),
        scratch_shapes=[pltpu.SemaphoreType.DMA, sems, sems, sems, sems, sems],
        compiler_params=pltpu.CompilerParams(
            collective_id=0, has_side_effects=True, vmem_limit_bytes=40 * 2**20
        ),
    )(own)


def cross_stack(sources, receivers):
    turned = jnp.stack([-sources[:, :, 1], sources[:, :, 0]], axis=2)
    paired = jnp.stack([sources, turned], axis=0)
    return jnp.einsum("jsgkf,rgkf->srjf", paired, receivers, preferred_element_type=jnp.float32)


def body(chan_count, raw_strain, bandpass, whiten_taps, segment_mask, channel_block, source_block):
    seg_count, chan_rows, sample_count = raw_strain.shape
    chan_start = lax.axis_index("chan") * chan_rows
    mask_all = segment_mask.astype(jnp.float32)
    mask_here = lax.dynamic_slice_in_dim(mask_all, chan_start, chan_rows, 1)
    spectra = front(raw_strain, bandpass, whiten_taps, mask_here)
    gathered = gather(spectra, chan_count).reshape(-1, seg_count, 2, FBINS)
    spectra = spectra.reshape(chan_rows, seg_count, 2, FBINS)
    member = channel_block == source_block[0]
    order = jnp.arange(member.shape[0], dtype=jnp.int32)
    below = member[None, :] & (order[None, :] < order[:, None])
    member_rank = jnp.sum(below.astype(jnp.int32), axis=1)
    chosen = member[None, :] & (member_rank[None, :] == jnp.arange(BLOCK, dtype=jnp.int32)[:, None])
    selector = chosen.astype(jnp.bfloat16)
    source_mask = jnp.dot(mask_all, chosen.astype(jnp.float32).T)
    counts = jnp.dot(source_mask.T, mask_here)
    sources = jnp.einsum(
        "sc,cgkf->sgkf",
        selector,
        gathered,
        preferred_element_type=jnp.float32,
    ).astype(jnp.bfloat16)
    stacked = cross_stack(sources, spectra).astype(jnp.bfloat16)
    lag_table = jnp.asarray(lag_table_np())
    lagged = jnp.dot(
        stacked.reshape(BLOCK * chan_rows, 2 * FBINS), lag_table, preferred_element_type=jnp.float32
    )
    lagged = lagged.reshape(BLOCK, chan_rows, LAGS)
    factor = 2.0 / (SAMPLES * math.sqrt(FBINS))
    return (lagged * factor / jnp.maximum(counts, 1.0)[:, :, None]).astype(jnp.bfloat16)


def solution(mesh):
    in_specs = (
        P(None, ("groups", "chan"), None),
        P(),
        P(("groups", "chan"), None),
        P(None, "groups"),
        P("groups"),
        P("groups"),
    )
    out_specs = P(None, ("groups", "chan"), None)
    return jax.shard_map(functools.partial(body, mesh.shape["chan"]), mesh=mesh, in_specs=in_specs, out_specs=out_specs, check_vma=False)
```

```python
import functools
import math

import jax
import numpy as np
import jax.numpy as jnp
from jax import lax
from jax.experimental import pallas as pl
from jax.experimental.pallas import tpu as pltpu
from jax.sharding import PartitionSpec as P

SAMPLES = 4096
KLO = 64
FBINS = 512
LAGS = 1024
BLOCK = 128


def table(phase):
    angles = phase.astype(np.float32) * np.float32(2.0 * math.pi / SAMPLES)
    return np.cos(angles).astype(jnp.bfloat16), (-np.sin(angles)).astype(jnp.bfloat16)


def dft_table():
    bins = KLO + np.arange(FBINS)
    return np.concatenate(table(np.arange(SAMPLES)[:, None] * bins[None, :] % SAMPLES), axis=1)


def lag_table_np():
    bins = KLO + np.arange(FBINS)
    return np.concatenate(table(bins[:, None] * (np.arange(LAGS) - LAGS // 2)[None, :] % SAMPLES), axis=0)


def toeplitz(taps):
    turned = pltpu.roll(jnp.broadcast_to(taps, (128, 128)), 0, 1, stride=1, stride_axis=0)
    row = lax.broadcasted_iota(jnp.int32, (128, 128), 0)
    lane = lax.broadcasted_iota(jnp.int32, (128, 128), 1)
    before = jnp.where(lane < row, turned, 0.0)
    here = jnp.where(lane >= row, turned, 0.0)
    return jnp.concatenate([before, here], axis=0).astype(jnp.bfloat16)


def front_kernel(raw_ref, band_ref, taps_ref, mask_ref, table_ref, out_ref, filt, inv, white, acc):
    segs, rows, samples = raw_ref.shape
    blocks = samples // 128
    step = pl.program_id(0)
    depth = table_ref.shape[0]

    @pl.when(step == 0)
    def _():
        matrix = toeplitz(band_ref[...])
        power = jnp.zeros((segs * rows, 128), jnp.float32)
        for b in range(blocks):
            if b == 0:
                joined = jnp.concatenate([raw_ref[:, :, samples - 128 :], raw_ref[:, :, :128]], axis=2)
            else:
                joined = raw_ref[:, :, (b - 1) * 128 : (b + 1) * 128]
            part = jnp.dot(joined.reshape(segs * rows, 256), matrix, preferred_element_type=jnp.float32)
            power = power + part * part
            filt[:, :, b * 128 : (b + 1) * 128] = part.reshape(segs, rows, 128)
        energy = jnp.sum(power, axis=1, keepdims=True) * (1.0 / samples)
        scale = 1.0 / jnp.sqrt(energy + 1e-05)
        inv[...] = jnp.broadcast_to(scale, (segs * rows, 128)).reshape(segs, rows, 128)
        for c in range(rows):
            matrix = toeplitz(taps_ref[c : c + 1, :])
            scale = inv[:, c, :]
            here = jnp.concatenate(
                [filt[:, c, b * 128 : (b + 1) * 128] * scale for b in range(blocks)], axis=0
            )
            before = jnp.concatenate([here[-segs:], here[:-segs]], axis=0)
            joined = jnp.concatenate([before, here], axis=1).astype(jnp.bfloat16)
            part = jnp.dot(joined, matrix, preferred_element_type=jnp.float32)
            for b in range(blocks):
                white[c * segs : (c + 1) * segs, b * 128 : (b + 1) * 128] = part[b * segs : (b + 1) * segs]
        acc[...] = jnp.zeros_like(acc)

    first = pl.multiple_of(step * depth, depth)
    acc[...] += jnp.dot(
        white[:, pl.ds(first, depth)].astype(jnp.bfloat16), table_ref[...], preferred_element_type=jnp.float32
    )

    @pl.when(step == pl.num_programs(0) - 1)
    def _():
        out_ref[...] = (acc[...] * mask_ref[...]).astype(jnp.bfloat16)


def front(raw, bandpass, whiten_taps, mask_here):
    segs, rows, samples = raw.shape
    pad = ((0, 0), (0, 128 - bandpass.shape[-1]))
    band = jnp.pad(bandpass.astype(jnp.float32)[None], pad)
    taps = jnp.pad(whiten_taps.astype(jnp.float32), pad)
    mask = mask_here.T.reshape(rows * segs, 1)
    depth = 512
    whole = lambda *shape: pl.BlockSpec(shape, lambda i: (0,) * len(shape))
    return pl.pallas_call(
        front_kernel,
        grid=(samples // depth,),
        out_shape=jax.ShapeDtypeStruct((rows * segs, 2 * FBINS), jnp.bfloat16),
        in_specs=[
            whole(segs, rows, samples),
            whole(1, 128),
            whole(rows, 128),
            whole(rows * segs, 1),
            pl.BlockSpec((depth, 2 * FBINS), lambda i: (i, 0)),
        ],
        out_specs=whole(rows * segs, 2 * FBINS),
        scratch_shapes=[
            pltpu.VMEM((segs, rows, samples), jnp.float32),
            pltpu.VMEM((segs, rows, 128), jnp.float32),
            pltpu.VMEM((rows * segs, samples), jnp.float32),
            pltpu.VMEM((rows * segs, 2 * FBINS), jnp.float32),
        ],
        compiler_params=pltpu.CompilerParams(vmem_limit_bytes=40 * 2**20),
        cost_estimate=pl.CostEstimate(flops=2 * 10**9, bytes_accessed=10**7, transcendentals=0),
    )(raw, band, taps, mask, jnp.asarray(dft_table()))


PIECES = 2


def gather_kernel(count, own_ref, out_ref, own_sem, up_sem, down_sem, y_sem, core_sem, recv_sem):
    levels = count // 4
    me = lax.axis_index("chan")
    level, side, core = me // 4, (me // 2) % 2, me % 2
    y_peer = me + 2 - 4 * side
    core_peer = me + 1 - 2 * core
    has_up, has_down = level < levels - 1, level > 0
    barrier = pltpu.get_barrier_semaphore()

    def greet(peer):
        pl.semaphore_signal(barrier, inc=1, device_id={"chan": peer}, device_id_type=pl.DeviceIdType.MESH)

    greet(y_peer)
    greet(core_peer)

    @pl.when(has_up)
    def _():
        greet(me + 4)

    @pl.when(has_down)
    def _():
        greet(me - 4)

    pl.semaphore_wait(barrier, 2 + has_up.astype(jnp.int32) + has_down.astype(jnp.int32))

    height = own_ref.shape[0] // PIECES

    def send(block, piece, sems, peer, source=None):
        rows = pl.ds(piece * height, height)
        place = out_ref.at[block, rows]
        return pltpu.make_async_remote_copy(
            src_ref=place if source is None else source.at[rows],
            dst_ref=place,
            send_sem=sems.at[block, piece],
            recv_sem=recv_sem.at[block, piece],
            device_id={"chan": peer},
            device_id_type=pl.DeviceIdType.MESH,
        )

    def arrived(block, piece):
        send(block, piece, y_sem, y_peer).wait_recv()

    keep = pltpu.make_async_copy(own_ref, out_ref.at[me], own_sem)
    keep.start()
    for piece in range(PIECES):

        @pl.when(has_up)
        def _():
            send(me, piece, up_sem, me + 4, own_ref).start()

        @pl.when(has_down)
        def _():
            send(me, piece, down_sem, me - 4, own_ref).start()

        send(me, piece, y_sem, y_peer, own_ref).start()
        send(me, piece, core_sem, core_peer, own_ref).start()

    def across(far):
        for piece in range(PIECES):
            block = far * 4 + (1 - side) * 2 + core
            arrived(block, piece)
            send(block, piece, core_sem, core_peer).start()

    def each(distance, act):
        for way in (1, -1):
            far = level + way * distance
            if distance == 0 and way == -1:
                continue

            @pl.when((far >= 0) & (far < levels))
            def _():
                act(far, way)

    for distance in range(1, levels + 1):
        if distance < levels:

            def along(far, way):
                block = far * 4 + side * 2 + core
                for piece in range(PIECES):
                    arrived(block, piece)
                    if way == 1:

                        @pl.when(has_down)
                        def _():
                            send(block, piece, down_sem, me - 4).start()
                    else:

                        @pl.when(has_up)
                        def _():
                            send(block, piece, up_sem, me + 4).start()

                    send(block, piece, y_sem, y_peer).start()
                    send(block, piece, core_sem, core_peer).start()

            each(distance, along)
        each(distance - 1, lambda far, way: across(far))

    for far in range(levels):
        for piece in range(PIECES):
            mine, other = far * 4 + side * 2 + core, far * 4 + (1 - side) * 2 + core
            arrived(far * 4 + side * 2 + 1 - core, piece)
            arrived(far * 4 + (1 - side) * 2 + 1 - core, piece)
            send(mine, piece, y_sem, y_peer).wait_send()
            send(mine, piece, core_sem, core_peer).wait_send()
            send(other, piece, core_sem, core_peer).wait_send()

            @pl.when(has_up & (far <= level))
            def _():
                send(mine, piece, up_sem, me + 4).wait_send()

            @pl.when(has_down & (far >= level))
            def _():
                send(mine, piece, down_sem, me - 4).wait_send()

    keep.wait()


def gather(own, count):
    if count % 4 or count < 4:
        return lax.all_gather(own, "chan", axis=0)
    sems = pltpu.SemaphoreType.DMA((count, PIECES))
    return pl.pallas_call(
        lambda *refs: gather_kernel(count, *refs),
        out_shape=jax.ShapeDtypeStruct((count,) + own.shape, own.dtype),
        in_specs=[pl.BlockSpec(memory_space=pltpu.VMEM)],
        out_specs=pl.BlockSpec(memory_space=pltpu.VMEM),
        scratch_shapes=[pltpu.SemaphoreType.DMA, sems, sems, sems, sems, sems],
        compiler_params=pltpu.CompilerParams(
            collective_id=0, has_side_effects=True, vmem_limit_bytes=40 * 2**20
        ),
    )(own)


SOURCES_STEP = 16


def back_kernel(index_ref, all_ref, own_ref, scale_ref, lag_ref, out_ref, local, first, stacked):
    rows, segs = local.shape[1], local.shape[0]
    step = pl.program_id(0)

    @pl.when(step == 0)
    def _():
        for r in range(0, rows, 2):
            pair = own_ref[r * segs : (r + 2) * segs].astype(jnp.float32)
            for k in range(2):
                for g in range(segs):
                    local[g, r + k : r + k + 1, :] = pair[k * segs + g : k * segs + g + 1]

    for s in range(SOURCES_STEP):
        channel = index_ref[step * SOURCES_STEP + s]
        pair = all_ref[pl.ds(pl.multiple_of((channel // 2) * 2 * segs, 2 * segs), 2 * segs), :]
        pair = pair.astype(jnp.float32)
        first[s] = jnp.where(channel % 2 == 0, pair[:segs], pair[segs:])

    for j in range(FBINS // 128):
        re, im = slice(j * 128, (j + 1) * 128), slice(FBINS + j * 128, FBINS + (j + 1) * 128)
        far = [(local[g, :, re], local[g, :, im]) for g in range(segs)]
        for s in range(SOURCES_STEP):
            total_re, total_im = 0.0, 0.0
            for g in range(segs):
                a = jnp.broadcast_to(first[s, g : g + 1, re], (rows, 128))
                b = jnp.broadcast_to(first[s, g : g + 1, im], (rows, 128))
                total_re = total_re + a * far[g][0] + b * far[g][1]
                total_im = total_im + a * far[g][1] - b * far[g][0]
            stacked[s * rows : (s + 1) * rows, re] = total_re.astype(jnp.bfloat16)
            stacked[s * rows : (s + 1) * rows, im] = total_im.astype(jnp.bfloat16)

    lagged = jnp.dot(stacked[...], lag_ref[...], preferred_element_type=jnp.float32) * scale_ref[...]
    out_ref[...] = lagged.astype(jnp.bfloat16).reshape(SOURCES_STEP, rows, LAGS)


def back(index, gathered, own, scale, rows, segs):
    width = 2 * FBINS
    once = lambda *shape: pl.BlockSpec(
        shape, lambda i, *_: (0,) * len(shape), pipeline_mode=pl.Buffered(1)
    )
    return pl.pallas_call(
        back_kernel,
        out_shape=jax.ShapeDtypeStruct((BLOCK, rows, LAGS), jnp.bfloat16),
        grid_spec=pltpu.PrefetchScalarGridSpec(
            num_scalar_prefetch=1,
            grid=(BLOCK // SOURCES_STEP,),
            in_specs=[
                once(*gathered.shape),
                once(*own.shape),
                pl.BlockSpec((SOURCES_STEP * rows, 1), lambda i, *_: (i, 0)),
                once(width, LAGS),
            ],
            out_specs=pl.BlockSpec((SOURCES_STEP, rows, LAGS), lambda i, *_: (i, 0, 0)),
            scratch_shapes=[
                pltpu.VMEM((segs, rows, width), jnp.float32),
                pltpu.VMEM((SOURCES_STEP, segs, width), jnp.float32),
                pltpu.VMEM((SOURCES_STEP * rows, width), jnp.bfloat16),
            ],
        ),
        compiler_params=pltpu.CompilerParams(vmem_limit_bytes=44 * 2**20),
        cost_estimate=pl.CostEstimate(flops=5 * 10**9, bytes_accessed=10**7, transcendentals=0),
    )(index, gathered, own, scale, jnp.asarray(lag_table_np()))


def body(chan_count, raw_strain, bandpass, whiten_taps, segment_mask, channel_block, source_block):
    seg_count, chan_rows, sample_count = raw_strain.shape
    chan_start = lax.axis_index("chan") * chan_rows
    mask_all = segment_mask.astype(jnp.float32)
    mask_here = lax.dynamic_slice_in_dim(mask_all, chan_start, chan_rows, 1)
    spectra = front(raw_strain, bandpass, whiten_taps, mask_here)
    gathered = gather(spectra, chan_count).reshape(-1, 2 * FBINS)
    member = channel_block == source_block[0]
    order = jnp.arange(member.shape[0], dtype=jnp.int32)
    below = member[None, :] & (order[None, :] < order[:, None])
    member_rank = jnp.sum(below.astype(jnp.int32), axis=1)
    chosen = member[None, :] & (member_rank[None, :] == jnp.arange(BLOCK, dtype=jnp.int32)[:, None])
    index = jnp.sum(jnp.where(chosen, order[None, :], 0), axis=1)
    source_mask = jnp.dot(mask_all, chosen.astype(jnp.float32).T)
    counts = jnp.dot(source_mask.T, mask_here)
    factor = 2.0 / (SAMPLES * math.sqrt(FBINS))
    scale = (factor / jnp.maximum(counts, 1.0)).reshape(BLOCK * chan_rows, 1)
    return back(index, gathered, spectra, scale, chan_rows, seg_count)


def solution(mesh):
    in_specs = (
        P(None, ("groups", "chan"), None),
        P(),
        P(("groups", "chan"), None),
        P(None, "groups"),
        P("groups"),
        P("groups"),
    )
    out_specs = P(None, ("groups", "chan"), None)
    return jax.shard_map(functools.partial(body, mesh.shape["chan"]), mesh=mesh, in_specs=in_specs, out_specs=out_specs, check_vma=False)
```

```python
import functools
import math

import jax
import numpy as np
import jax.numpy as jnp
from jax import lax
from jax.experimental import pallas as pl
from jax.experimental.pallas import tpu as pltpu
from jax.sharding import PartitionSpec as P

SAMPLES = 4096
KLO = 64
FBINS = 512
LAGS = 1024
BLOCK = 128


def table(phase):
    angles = phase.astype(np.float32) * np.float32(2.0 * math.pi / SAMPLES)
    return np.cos(angles).astype(jnp.bfloat16), (-np.sin(angles)).astype(jnp.bfloat16)


def dft_table():
    bins = KLO + np.arange(FBINS)
    return np.concatenate(table(np.arange(SAMPLES)[:, None] * bins[None, :] % SAMPLES), axis=1)


def lag_table_np():
    bins = KLO + np.arange(FBINS)
    return np.concatenate(table(bins[:, None] * (np.arange(LAGS) - LAGS // 2)[None, :] % SAMPLES), axis=0)


def toeplitz(taps):
    turned = pltpu.roll(jnp.broadcast_to(taps, (128, 128)), 0, 1, stride=1, stride_axis=0)
    row = lax.broadcasted_iota(jnp.int32, (128, 128), 0)
    lane = lax.broadcasted_iota(jnp.int32, (128, 128), 1)
    before = jnp.where(lane < row, turned, 0.0)
    here = jnp.where(lane >= row, turned, 0.0)
    return jnp.concatenate([before, here], axis=0).astype(jnp.bfloat16)


def front_kernel(raw_ref, band_ref, taps_ref, mask_ref, table_ref, out_ref, filt, inv, white, acc):
    segs, rows, samples = raw_ref.shape
    blocks = samples // 128
    step = pl.program_id(0)
    depth = table_ref.shape[0]

    @pl.when(step == 0)
    def _():
        widen = lambda x: jnp.pad(x.astype(jnp.float32), ((0, 0), (0, 128 - x.shape[1])))
        matrix = toeplitz(widen(band_ref[...]))
        taps = widen(taps_ref[...])
        power = jnp.zeros((segs * rows, 128), jnp.float32)
        for b in range(blocks):
            if b == 0:
                joined = jnp.concatenate([raw_ref[:, :, samples - 128 :], raw_ref[:, :, :128]], axis=2)
            else:
                joined = raw_ref[:, :, (b - 1) * 128 : (b + 1) * 128]
            part = jnp.dot(joined.reshape(segs * rows, 256), matrix, preferred_element_type=jnp.float32)
            power = power + part * part
            filt[:, :, b * 128 : (b + 1) * 128] = part.reshape(segs, rows, 128)
        energy = jnp.sum(power, axis=1, keepdims=True) * (1.0 / samples)
        scale = 1.0 / jnp.sqrt(energy + 1e-05)
        inv[...] = jnp.broadcast_to(scale, (segs * rows, 128)).reshape(segs, rows, 128)
        for c in range(rows):
            matrix = toeplitz(taps[c : c + 1, :])
            scale = inv[:, c, :]
            here = jnp.concatenate(
                [filt[:, c, b * 128 : (b + 1) * 128] * scale for b in range(blocks)], axis=0
            )
            before = jnp.concatenate([here[-segs:], here[:-segs]], axis=0)
            joined = jnp.concatenate([before, here], axis=1).astype(jnp.bfloat16)
            part = jnp.dot(joined, matrix, preferred_element_type=jnp.float32)
            for b in range(blocks):
                white[c * segs : (c + 1) * segs, b * 128 : (b + 1) * 128] = part[b * segs : (b + 1) * segs]
        acc[...] = jnp.zeros_like(acc)

    first = pl.multiple_of(step * depth, depth)
    acc[...] += jnp.dot(
        white[:, pl.ds(first, depth)].astype(jnp.bfloat16), table_ref[...], preferred_element_type=jnp.float32
    )

    @pl.when(step == pl.num_programs(0) - 1)
    def _():
        out_ref[...] = (acc[...] * mask_ref[...]).astype(jnp.bfloat16)


def front(raw, bandpass, whiten_taps, mask_here):
    segs, rows, samples = raw.shape
    band, taps = bandpass[None], whiten_taps
    mask = mask_here.T.reshape(rows * segs, 1)
    depth = 512
    whole = lambda *shape: pl.BlockSpec(shape, lambda i: (0,) * len(shape))
    return pl.pallas_call(
        front_kernel,
        grid=(samples // depth,),
        out_shape=jax.ShapeDtypeStruct((rows * segs, 2 * FBINS), jnp.bfloat16),
        in_specs=[
            whole(segs, rows, samples),
            whole(*band.shape),
            whole(*taps.shape),
            whole(rows * segs, 1),
            pl.BlockSpec((depth, 2 * FBINS), lambda i: (i, 0)),
        ],
        out_specs=whole(rows * segs, 2 * FBINS),
        scratch_shapes=[
            pltpu.VMEM((segs, rows, samples), jnp.float32),
            pltpu.VMEM((segs, rows, 128), jnp.float32),
            pltpu.VMEM((rows * segs, samples), jnp.float32),
            pltpu.VMEM((rows * segs, 2 * FBINS), jnp.float32),
        ],
        compiler_params=pltpu.CompilerParams(vmem_limit_bytes=56 * 2**20),
        cost_estimate=pl.CostEstimate(flops=2 * 10**9, bytes_accessed=10**7, transcendentals=0),
    )(raw, band, taps, mask, jnp.asarray(dft_table()))


PIECES = 4


def gather_kernel(count, own_ref, out_ref, own_sem, up_sem, down_sem, y_sem, core_sem, recv_sem):
    levels = count // 4
    me = lax.axis_index("chan")
    level, side, core = me // 4, (me // 2) % 2, me % 2
    y_peer = me + 2 - 4 * side
    core_peer = me + 1 - 2 * core
    has_up, has_down = level < levels - 1, level > 0
    barrier = pltpu.get_barrier_semaphore()

    def greet(peer):
        pl.semaphore_signal(barrier, inc=1, device_id={"chan": peer}, device_id_type=pl.DeviceIdType.MESH)

    greet(y_peer)
    greet(core_peer)

    @pl.when(has_up)
    def _():
        greet(me + 4)

    @pl.when(has_down)
    def _():
        greet(me - 4)

    pl.semaphore_wait(barrier, 2 + has_up.astype(jnp.int32) + has_down.astype(jnp.int32))

    height = own_ref.shape[0] // PIECES

    def send(block, piece, sems, peer, source=None):
        rows = pl.ds(piece * height, height)
        place = out_ref.at[block, rows]
        return pltpu.make_async_remote_copy(
            src_ref=place if source is None else source.at[rows],
            dst_ref=place,
            send_sem=sems.at[block, piece],
            recv_sem=recv_sem.at[block, piece],
            device_id={"chan": peer},
            device_id_type=pl.DeviceIdType.MESH,
        )

    def arrived(block, piece):
        send(block, piece, y_sem, y_peer).wait_recv()

    keep = pltpu.make_async_copy(own_ref, out_ref.at[me], own_sem)
    keep.start()
    for piece in range(PIECES):

        @pl.when(has_up)
        def _():
            send(me, piece, up_sem, me + 4, own_ref).start()

        @pl.when(has_down)
        def _():
            send(me, piece, down_sem, me - 4, own_ref).start()

        send(me, piece, y_sem, y_peer, own_ref).start()
        send(me, piece, core_sem, core_peer, own_ref).start()

    def across(far, way, piece):
        block = far * 4 + (1 - side) * 2 + core
        arrived(block, piece)
        send(block, piece, core_sem, core_peer).start()

    def along(far, way, piece):
        block = far * 4 + side * 2 + core
        arrived(block, piece)

        @pl.when(has_down if way == 1 else has_up)
        def _():
            sems, peer = (down_sem, me - 4) if way == 1 else (up_sem, me + 4)
            send(block, piece, sems, peer).start()

        send(block, piece, y_sem, y_peer).start()
        send(block, piece, core_sem, core_peer).start()

    def each(distance, piece, act):
        for way in (1, -1) if distance else (1,):
            far = level + way * distance

            @pl.when((far >= 0) & (far < levels))
            def _():
                act(far, way, piece)

    for distance in range(1, levels + 1):
        for piece in range(PIECES):
            if distance < levels:
                each(distance, piece, along)
            each(distance - 1, piece, across)

    for far in range(levels):
        for piece in range(PIECES):
            mine, other = far * 4 + side * 2 + core, far * 4 + (1 - side) * 2 + core
            arrived(far * 4 + side * 2 + 1 - core, piece)
            arrived(far * 4 + (1 - side) * 2 + 1 - core, piece)
            send(mine, piece, y_sem, y_peer).wait_send()
            send(mine, piece, core_sem, core_peer).wait_send()
            send(other, piece, core_sem, core_peer).wait_send()

            @pl.when(has_up & (far <= level))
            def _():
                send(mine, piece, up_sem, me + 4).wait_send()

            @pl.when(has_down & (far >= level))
            def _():
                send(mine, piece, down_sem, me - 4).wait_send()

    keep.wait()


def gather(own, count):
    if count % 4 or count < 4:
        return lax.all_gather(own, "chan", axis=0)
    sems = pltpu.SemaphoreType.DMA((count, PIECES))
    return pl.pallas_call(
        lambda *refs: gather_kernel(count, *refs),
        out_shape=jax.ShapeDtypeStruct((count,) + own.shape, own.dtype),
        in_specs=[pl.BlockSpec(memory_space=pltpu.VMEM)],
        out_specs=pl.BlockSpec(memory_space=pltpu.VMEM),
        scratch_shapes=[pltpu.SemaphoreType.DMA, sems, sems, sems, sems, sems],
        compiler_params=pltpu.CompilerParams(
            collective_id=0, has_side_effects=True, vmem_limit_bytes=40 * 2**20
        ),
    )(own)


CHUNK = 16
SOURCES_STEP = 2 * CHUNK


def back_kernel(index_ref, all_ref, own_ref, scale_ref, lag_ref, out_ref, local, first, stacked_a, stacked_b):
    rows, segs = local.shape[1], local.shape[0]
    step = pl.program_id(0)

    @pl.when(step == 0)
    def _():
        for r in range(0, rows, 2):
            pair = own_ref[r * segs : (r + 2) * segs].astype(jnp.float32)
            for k in range(2):
                for g in range(segs):
                    local[g, r + k : r + k + 1, :] = pair[k * segs + g : k * segs + g + 1]

    for chunk, stacked in enumerate((stacked_a, stacked_b)):
        base = chunk * CHUNK
        for s in range(CHUNK):
            channel = index_ref[step * SOURCES_STEP + base + s]
            pair = all_ref[pl.ds(pl.multiple_of((channel // 2) * 2 * segs, 2 * segs), 2 * segs), :]
            pair = pair.astype(jnp.float32)
            first[base + s] = jnp.where(channel % 2 == 0, pair[:segs], pair[segs:])
        for j in range(FBINS // 128):
            re, im = slice(j * 128, (j + 1) * 128), slice(FBINS + j * 128, FBINS + (j + 1) * 128)
            far = [(local[g, :, re], local[g, :, im]) for g in range(segs)]
            for s in range(CHUNK):
                total_re, total_im = 0.0, 0.0
                for g in range(segs):
                    a = jnp.broadcast_to(first[base + s, g : g + 1, re], (rows, 128))
                    b = jnp.broadcast_to(first[base + s, g : g + 1, im], (rows, 128))
                    total_re = total_re + a * far[g][0] + b * far[g][1]
                    total_im = total_im + a * far[g][1] - b * far[g][0]
                stacked[s * rows : (s + 1) * rows, re] = total_re.astype(jnp.bfloat16)
                stacked[s * rows : (s + 1) * rows, im] = total_im.astype(jnp.bfloat16)
        lagged = jnp.dot(stacked[...], lag_ref[...], preferred_element_type=jnp.float32)
        lagged = lagged * scale_ref[base * rows : (base + CHUNK) * rows]
        out_ref[base : base + CHUNK] = lagged.astype(jnp.bfloat16).reshape(CHUNK, rows, LAGS)


def back(index, gathered, own, scale, rows, segs):
    width = 2 * FBINS
    once = lambda *shape: pl.BlockSpec(
        shape, lambda i, *_: (0,) * len(shape), pipeline_mode=pl.Buffered(1)
    )
    return pl.pallas_call(
        back_kernel,
        out_shape=jax.ShapeDtypeStruct((BLOCK, rows, LAGS), jnp.bfloat16),
        grid_spec=pltpu.PrefetchScalarGridSpec(
            num_scalar_prefetch=1,
            grid=(BLOCK // SOURCES_STEP,),
            in_specs=[
                once(*gathered.shape),
                once(*own.shape),
                pl.BlockSpec((SOURCES_STEP * rows, 1), lambda i, *_: (i, 0)),
                once(width, LAGS),
            ],
            out_specs=pl.BlockSpec((SOURCES_STEP, rows, LAGS), lambda i, *_: (i, 0, 0)),
            scratch_shapes=[
                pltpu.VMEM((segs, rows, width), jnp.float32),
                pltpu.VMEM((SOURCES_STEP, segs, width), jnp.float32),
                pltpu.VMEM((CHUNK * rows, width), jnp.bfloat16),
                pltpu.VMEM((CHUNK * rows, width), jnp.bfloat16),
            ],
        ),
        compiler_params=pltpu.CompilerParams(vmem_limit_bytes=44 * 2**20),
        cost_estimate=pl.CostEstimate(flops=5 * 10**9, bytes_accessed=10**7, transcendentals=0),
    )(index, gathered, own, scale, jnp.asarray(lag_table_np()))


def body(chan_count, raw_strain, bandpass, whiten_taps, segment_mask, channel_block, source_block):
    seg_count, chan_rows, sample_count = raw_strain.shape
    chan_start = lax.axis_index("chan") * chan_rows
    mask_all = segment_mask.astype(jnp.float32)
    mask_here = lax.dynamic_slice_in_dim(mask_all, chan_start, chan_rows, 1)
    spectra = front(raw_strain, bandpass, whiten_taps, mask_here)
    gathered = gather(spectra, chan_count).reshape(-1, 2 * FBINS)
    member = channel_block == source_block[0]
    order = jnp.arange(member.shape[0], dtype=jnp.int32)
    below = member[None, :] & (order[None, :] < order[:, None])
    member_rank = jnp.sum(below.astype(jnp.int32), axis=1)
    chosen = member[None, :] & (member_rank[None, :] == jnp.arange(BLOCK, dtype=jnp.int32)[:, None])
    index = jnp.sum(jnp.where(chosen, order[None, :], 0), axis=1)
    source_mask = jnp.dot(mask_all, chosen.astype(jnp.float32).T)
    counts = jnp.dot(source_mask.T, mask_here)
    factor = 2.0 / (SAMPLES * math.sqrt(FBINS))
    scale = (factor / jnp.maximum(counts, 1.0)).reshape(BLOCK * chan_rows, 1)
    return back(index, gathered, spectra, scale, chan_rows, seg_count)


def solution(mesh):
    in_specs = (
        P(None, ("groups", "chan"), None),
        P(),
        P(("groups", "chan"), None),
        P(None, "groups"),
        P("groups"),
        P("groups"),
    )
    out_specs = P(None, ("groups", "chan"), None)
    return jax.shard_map(functools.partial(body, mesh.shape["chan"]), mesh=mesh, in_specs=in_specs, out_specs=out_specs, check_vma=False)
```

```python
import functools
import math

import jax
import numpy as np
import jax.numpy as jnp
from jax import lax
from jax.experimental import pallas as pl
from jax.experimental.pallas import tpu as pltpu
from jax.sharding import PartitionSpec as P

SAMPLES = 4096
KLO = 64
FBINS = 512
LAGS = 1024
BLOCK = 128


def table(phase):
    angles = phase.astype(np.float32) * np.float32(2.0 * math.pi / SAMPLES)
    return np.cos(angles).astype(jnp.bfloat16), (-np.sin(angles)).astype(jnp.bfloat16)


def bin_order():
    bins = KLO + np.arange(FBINS)
    return np.concatenate([bins[bins % 2 == 0], bins[bins % 2 == 1]])


def dft_table():
    even, odd = np.split(bin_order(), 2)
    time = np.arange(SAMPLES // 2)[:, None]
    return np.concatenate(table(time * even % SAMPLES) + table(time * odd % SAMPLES), axis=1)


def lag_table_np():
    return np.concatenate(table(bin_order()[:, None] * (np.arange(LAGS) - LAGS // 2)[None, :] % SAMPLES), axis=0)


def toeplitz(taps):
    turned = pltpu.roll(jnp.broadcast_to(taps, (128, 128)), 0, 1, stride=1, stride_axis=0)
    row = lax.broadcasted_iota(jnp.int32, (128, 128), 0)
    lane = lax.broadcasted_iota(jnp.int32, (128, 128), 1)
    before = jnp.where(lane < row, turned, 0.0)
    here = jnp.where(lane >= row, turned, 0.0)
    return jnp.concatenate([before, here], axis=0).astype(jnp.bfloat16)


def front_kernel(raw_ref, band_ref, taps_ref, mask_ref, table_ref, out_ref, filt, inv, white, acc):
    segs, rows, samples = raw_ref.shape
    blocks = samples // 128
    step = pl.program_id(0)
    depth = table_ref.shape[0]

    @pl.when(step == 0)
    def _():
        widen = lambda x: jnp.pad(x.astype(jnp.float32), ((0, 0), (0, 128 - x.shape[1])))
        matrix = toeplitz(widen(band_ref[...]))
        taps = widen(taps_ref[...])
        power = jnp.zeros((segs * rows, 128), jnp.float32)
        for b in range(blocks):
            if b == 0:
                joined = jnp.concatenate([raw_ref[:, :, samples - 128 :], raw_ref[:, :, :128]], axis=2)
            else:
                joined = raw_ref[:, :, (b - 1) * 128 : (b + 1) * 128]
            part = jnp.dot(joined.reshape(segs * rows, 256), matrix, preferred_element_type=jnp.float32)
            power = power + part * part
            filt[:, :, b * 128 : (b + 1) * 128] = part.reshape(segs, rows, 128)
        energy = jnp.sum(power, axis=1, keepdims=True) * (1.0 / samples)
        scale = 1.0 / jnp.sqrt(energy + 1e-05)
        inv[...] = jnp.broadcast_to(scale, (segs * rows, 128)).reshape(segs, rows, 128)
        for c in range(rows):
            matrix = toeplitz(taps[c : c + 1, :])
            scale = inv[:, c, :]
            here = jnp.concatenate(
                [filt[:, c, b * 128 : (b + 1) * 128] * scale for b in range(blocks)], axis=0
            )
            before = jnp.concatenate([here[-segs:], here[:-segs]], axis=0)
            joined = jnp.concatenate([before, here], axis=1).astype(jnp.bfloat16)
            part = jnp.dot(joined, matrix, preferred_element_type=jnp.float32)
            for b in range(blocks):
                white[c * segs : (c + 1) * segs, b * 128 : (b + 1) * 128] = part[b * segs : (b + 1) * segs]
        acc[...] = jnp.zeros_like(acc)

    first = pl.multiple_of(step * depth, depth)
    early = white[:, pl.ds(first, depth)].astype(jnp.bfloat16).astype(jnp.float32)
    late = white[:, pl.ds(pl.multiple_of(first + samples // 2, depth), depth)].astype(jnp.bfloat16).astype(jnp.float32)
    for odd, folded in enumerate((early + late, early - late)):
        part = jnp.dot(
            folded.astype(jnp.bfloat16),
            table_ref[:, odd * FBINS : (odd + 1) * FBINS],
            preferred_element_type=jnp.float32,
        )
        half = FBINS // 2
        acc[:, odd * half : (odd + 1) * half] += part[:, :half]
        acc[:, FBINS + odd * half : FBINS + (odd + 1) * half] += part[:, half:]

    @pl.when(step == pl.num_programs(0) - 1)
    def _():
        out_ref[...] = (acc[...] * mask_ref[...]).astype(jnp.bfloat16)


def front(raw, bandpass, whiten_taps, mask_here):
    segs, rows, samples = raw.shape
    band, taps = bandpass[None], whiten_taps
    mask = mask_here.T.reshape(rows * segs, 1)
    depth = 512
    whole = lambda *shape: pl.BlockSpec(shape, lambda i: (0,) * len(shape))
    return pl.pallas_call(
        front_kernel,
        grid=(samples // 2 // depth,),
        out_shape=jax.ShapeDtypeStruct((rows * segs, 2 * FBINS), jnp.bfloat16),
        in_specs=[
            whole(segs, rows, samples),
            whole(*band.shape),
            whole(*taps.shape),
            whole(rows * segs, 1),
            pl.BlockSpec((depth, 2 * FBINS), lambda i: (i, 0)),
        ],
        out_specs=whole(rows * segs, 2 * FBINS),
        scratch_shapes=[
            pltpu.VMEM((segs, rows, samples), jnp.float32),
            pltpu.VMEM((segs, rows, 128), jnp.float32),
            pltpu.VMEM((rows * segs, samples), jnp.float32),
            pltpu.VMEM((rows * segs, 2 * FBINS), jnp.float32),
        ],
        compiler_params=pltpu.CompilerParams(vmem_limit_bytes=40 * 2**20),
        cost_estimate=pl.CostEstimate(flops=2 * 10**9, bytes_accessed=10**7, transcendentals=0),
    )(raw, band, taps, mask, jnp.asarray(dft_table()))


PIECES = 2


def gather_kernel(count, own_ref, out_ref, own_sem, up_sem, down_sem, y_sem, core_sem, recv_sem):
    levels = count // 4
    me = lax.axis_index("chan")
    level, side, core = me // 4, (me // 2) % 2, me % 2
    y_peer = me + 2 - 4 * side
    core_peer = me + 1 - 2 * core
    has_up, has_down = level < levels - 1, level > 0
    barrier = pltpu.get_barrier_semaphore()

    def greet(peer):
        pl.semaphore_signal(barrier, inc=1, device_id={"chan": peer}, device_id_type=pl.DeviceIdType.MESH)

    greet(y_peer)
    greet(core_peer)

    @pl.when(has_up)
    def _():
        greet(me + 4)

    @pl.when(has_down)
    def _():
        greet(me - 4)

    pl.semaphore_wait(barrier, 2 + has_up.astype(jnp.int32) + has_down.astype(jnp.int32))

    height = own_ref.shape[0] // PIECES

    def send(block, piece, sems, peer, source=None):
        rows = pl.ds(piece * height, height)
        place = out_ref.at[block, rows]
        return pltpu.make_async_remote_copy(
            src_ref=place if source is None else source.at[rows],
            dst_ref=place,
            send_sem=sems.at[block, piece],
            recv_sem=recv_sem.at[block, piece],
            device_id={"chan": peer},
            device_id_type=pl.DeviceIdType.MESH,
        )

    def arrived(block, piece):
        send(block, piece, y_sem, y_peer).wait_recv()

    keep = pltpu.make_async_copy(own_ref, out_ref.at[me], own_sem)
    keep.start()
    for piece in range(PIECES):

        @pl.when(has_up)
        def _():
            send(me, piece, up_sem, me + 4, own_ref).start()

        @pl.when(has_down)
        def _():
            send(me, piece, down_sem, me - 4, own_ref).start()

        send(me, piece, y_sem, y_peer, own_ref).start()
        send(me, piece, core_sem, core_peer, own_ref).start()

    def across(far, way, piece):
        block = far * 4 + (1 - side) * 2 + core
        arrived(block, piece)
        send(block, piece, core_sem, core_peer).start()

    def along(far, way, piece):
        block = far * 4 + side * 2 + core
        arrived(block, piece)

        @pl.when(has_down if way == 1 else has_up)
        def _():
            sems, peer = (down_sem, me - 4) if way == 1 else (up_sem, me + 4)
            send(block, piece, sems, peer).start()

        send(block, piece, y_sem, y_peer).start()
        send(block, piece, core_sem, core_peer).start()

    def each(distance, piece, act):
        for way in (1, -1) if distance else (1,):
            far = level + way * distance

            @pl.when((far >= 0) & (far < levels))
            def _():
                act(far, way, piece)

    for distance in range(1, levels + 1):
        for piece in range(PIECES):
            if distance < levels:
                each(distance, piece, along)
            each(distance - 1, piece, across)

    for far in range(levels):
        for piece in range(PIECES):
            mine, other = far * 4 + side * 2 + core, far * 4 + (1 - side) * 2 + core
            arrived(far * 4 + side * 2 + 1 - core, piece)
            arrived(far * 4 + (1 - side) * 2 + 1 - core, piece)
            send(mine, piece, y_sem, y_peer).wait_send()
            send(mine, piece, core_sem, core_peer).wait_send()
            send(other, piece, core_sem, core_peer).wait_send()

            @pl.when(has_up & (far <= level))
            def _():
                send(mine, piece, up_sem, me + 4).wait_send()

            @pl.when(has_down & (far >= level))
            def _():
                send(mine, piece, down_sem, me - 4).wait_send()

    keep.wait()


def gather(own, count):
    if count % 4 or count < 4:
        return lax.all_gather(own, "chan", axis=0)
    sems = pltpu.SemaphoreType.DMA((count, PIECES))
    return pl.pallas_call(
        lambda *refs: gather_kernel(count, *refs),
        out_shape=jax.ShapeDtypeStruct((count,) + own.shape, own.dtype),
        in_specs=[pl.BlockSpec(memory_space=pltpu.VMEM)],
        out_specs=pl.BlockSpec(memory_space=pltpu.VMEM),
        scratch_shapes=[pltpu.SemaphoreType.DMA, sems, sems, sems, sems, sems],
        compiler_params=pltpu.CompilerParams(
            collective_id=0, has_side_effects=True, vmem_limit_bytes=40 * 2**20
        ),
    )(own)


CHUNK = 16
SOURCES_STEP = 2 * CHUNK


def back_kernel(index_ref, all_ref, own_ref, scale_ref, lag_ref, out_ref, local, first, stacked_a, stacked_b):
    rows, segs = local.shape[1], local.shape[0]
    step = pl.program_id(0)

    @pl.when(step == 0)
    def _():
        for r in range(0, rows, 2):
            pair = own_ref[r * segs : (r + 2) * segs].astype(jnp.float32)
            for k in range(2):
                for g in range(segs):
                    local[g, r + k : r + k + 1, :] = pair[k * segs + g : k * segs + g + 1]

    for chunk, stacked in enumerate((stacked_a, stacked_b)):
        base = chunk * CHUNK
        for s in range(CHUNK):
            channel = index_ref[step * SOURCES_STEP + base + s]
            pair = all_ref[pl.ds(pl.multiple_of((channel // 2) * 2 * segs, 2 * segs), 2 * segs), :]
            pair = pair.astype(jnp.float32)
            first[base + s] = jnp.where(channel % 2 == 0, pair[:segs], pair[segs:])
        for j in range(FBINS // 128):
            re, im = slice(j * 128, (j + 1) * 128), slice(FBINS + j * 128, FBINS + (j + 1) * 128)
            far = [(local[g, :, re], local[g, :, im]) for g in range(segs)]
            for s in range(CHUNK):
                total_re, total_im = 0.0, 0.0
                for g in range(segs):
                    a = jnp.broadcast_to(first[base + s, g : g + 1, re], (rows, 128))
                    b = jnp.broadcast_to(first[base + s, g : g + 1, im], (rows, 128))
                    total_re = total_re + a * far[g][0] + b * far[g][1]
                    total_im = total_im + a * far[g][1] - b * far[g][0]
                stacked[s * rows : (s + 1) * rows, re] = total_re.astype(jnp.bfloat16)
                stacked[s * rows : (s + 1) * rows, im] = total_im.astype(jnp.bfloat16)
        lagged = jnp.dot(stacked[...], lag_ref[...], preferred_element_type=jnp.float32)
        lagged = lagged * scale_ref[base * rows : (base + CHUNK) * rows]
        out_ref[base : base + CHUNK] = lagged.astype(jnp.bfloat16).reshape(CHUNK, rows, LAGS)


def back(index, gathered, own, scale, rows, segs):
    width = 2 * FBINS
    once = lambda *shape: pl.BlockSpec(
        shape, lambda i, *_: (0,) * len(shape), pipeline_mode=pl.Buffered(1)
    )
    return pl.pallas_call(
        back_kernel,
        out_shape=jax.ShapeDtypeStruct((BLOCK, rows, LAGS), jnp.bfloat16),
        grid_spec=pltpu.PrefetchScalarGridSpec(
            num_scalar_prefetch=1,
            grid=(BLOCK // SOURCES_STEP,),
            in_specs=[
                once(*gathered.shape),
                once(*own.shape),
                pl.BlockSpec((SOURCES_STEP * rows, 1), lambda i, *_: (i, 0)),
                once(width, LAGS),
            ],
            out_specs=pl.BlockSpec((SOURCES_STEP, rows, LAGS), lambda i, *_: (i, 0, 0)),
            scratch_shapes=[
                pltpu.VMEM((segs, rows, width), jnp.float32),
                pltpu.VMEM((SOURCES_STEP, segs, width), jnp.float32),
                pltpu.VMEM((CHUNK * rows, width), jnp.bfloat16),
                pltpu.VMEM((CHUNK * rows, width), jnp.bfloat16),
            ],
        ),
        compiler_params=pltpu.CompilerParams(vmem_limit_bytes=44 * 2**20),
        cost_estimate=pl.CostEstimate(flops=5 * 10**9, bytes_accessed=10**7, transcendentals=0),
    )(index, gathered, own, scale, jnp.asarray(lag_table_np()))


def body(chan_count, raw_strain, bandpass, whiten_taps, segment_mask, channel_block, source_block):
    seg_count, chan_rows, sample_count = raw_strain.shape
    chan_start = lax.axis_index("chan") * chan_rows
    mask_all = segment_mask.astype(jnp.float32)
    mask_here = lax.dynamic_slice_in_dim(mask_all, chan_start, chan_rows, 1)
    spectra = front(raw_strain, bandpass, whiten_taps, mask_here)
    gathered = gather(spectra, chan_count).reshape(-1, 2 * FBINS)
    member = channel_block == source_block[0]
    order = jnp.arange(member.shape[0], dtype=jnp.int32)
    below = member[None, :] & (order[None, :] < order[:, None])
    member_rank = jnp.sum(below.astype(jnp.int32), axis=1)
    chosen = member[None, :] & (member_rank[None, :] == jnp.arange(BLOCK, dtype=jnp.int32)[:, None])
    index = jnp.sum(jnp.where(chosen, order[None, :], 0), axis=1)
    source_mask = jnp.dot(mask_all, chosen.astype(jnp.float32).T)
    counts = jnp.dot(source_mask.T, mask_here)
    factor = 2.0 / (SAMPLES * math.sqrt(FBINS))
    scale = (factor / jnp.maximum(counts, 1.0)).reshape(BLOCK * chan_rows, 1)
    return back(index, gathered, spectra, scale, chan_rows, seg_count)


def solution(mesh):
    in_specs = (
        P(None, ("groups", "chan"), None),
        P(),
        P(("groups", "chan"), None),
        P(None, "groups"),
        P("groups"),
        P("groups"),
    )
    out_specs = P(None, ("groups", "chan"), None)
    return jax.shard_map(functools.partial(body, mesh.shape["chan"]), mesh=mesh, in_specs=in_specs, out_specs=out_specs, check_vma=False)
```
